32 devices in a mesh: grp: 2 (over y), depth: 4 (over z), shot: 2 (over x), lat: 2 (over core).
Axes of the slice: x: 2, y: 2, z: 4, core: 2. Of those that a mesh axis runs over, the one named last changes fastest.
Arguments:
- fwd_prev: float32 [8, 8, 128, 128], P(('grp', 'shot'), 'depth', 'lat'), parts along dimension 0, may hold values from -6 to 6
- fwd_now: float32 [8, 8, 128, 128], P(('grp', 'shot'), 'depth', 'lat'), parts along dimension 0, may hold values from -6 to 6
- adj_late: float32 [8, 8, 128, 128], P(('grp', 'shot'), 'depth', 'lat'), parts along dimension 0, may hold values from -6 to 6
- adj_last: float32 [8, 8, 128, 128], P(('grp', 'shot'), 'depth', 'lat'), parts along dimension 0, may hold values from -6 to 6
- velocity: float32 [16, 128, 128], P(('grp', 'depth'), 'lat', 'shot'), parts along dimension 0, may hold values from 1.5 to 4.5
- density: float32 [16, 128, 128], P(('grp', 'depth'), 'lat'), parts along dimension 0, may hold values from 1.5 to 2.5
- wavelet: float32 [8, 2], P(('grp', 'shot')), parts along dimension 0, may hold values from -48 to 48
- source_cell: int32 [8], P(('grp', 'shot')), parts along dimension 0, may hold values from 0 to 131071
- receiver_cell: int32 [8, 2048], P(('grp', 'shot')), parts along dimension 0, may hold values from 0 to 131071
- observed: float32 [8, 2, 2048], P(('grp', 'shot')), parts along dimension 0, may hold values from -18 to 18
Outputs:
- updated_velocity: float32 [16, 128, 128], P(('grp', 'depth'), 'lat', 'shot'), parts along dimension 0
- update_direction: float32 [16, 128, 128], P(('grp', 'depth'), 'lat', 'shot'), parts along dimension 0
The draws below stay inside these ranges and needn't reach their ends.
There are 2 independent parts, one for each index of `grp`. The reference program is written for one: setup_inputs(seed, part) draws one part's arguments, and reference() takes and returns one part's arrays. A program takes and returns all parts, laid end to end along the dimension named above; each array names one. Nothing has to cross between parts.
Inputs may be any that keep to these rules, and one draw needn't show every extreme that they name: `source_cell`: a flattened cell index depth * 128 * 128 + x * 128 + y. `receiver_cell`: flattened cell indices depth * 128 * 128 + x * 128 + y; a cell may repeat.
All inputs are finite; a program needn't handle non-finite values. Where the reference program divides by a largest or mean magnitude, that divisor is 1e-20 or more.
Results may differ from the reference program's by a relative error of at most 0.00002.
Values sent between devices are 32-bit elements; how exact they have to be, the bound alone decides.
A program may use at most 64 MiB of HBM per device.

```python
import jax
import jax.numpy as jnp
from jax import lax

NY = 128
NREC = 2048
STEPS = 2
ITERS = 2
NZ = 8
NX = 128
SHOTS = 4


def place_ends(drawn, own_key, low, high):
    index_at = [jax.random.randint(jax.random.fold_in(own_key, axis), (), 0, length) for axis, length in enumerate(drawn.shape)]
    longest = drawn.shape.index(max(drawn.shape))
    neighbour = index_at[:longest] + [(index_at[longest] + 1) % drawn.shape[longest]] + index_at[longest + 1:]
    return drawn.at[tuple(index_at)].set(low).at[tuple(neighbour)].set(high)


def level_of(own_key, dims, shards, low, top_value):
    gain, own = 1.0, jax.random.fold_in(own_key, 6)
    for position, blocks in shards:
        heights = jnp.exp(jax.random.uniform(jax.random.fold_in(own, position), (blocks,), jnp.float32, low / len(shards), top_value / len(shards)))
        gain = gain * jnp.repeat(heights, dims[position] // blocks).reshape([-1 if axis == position else 1 for axis in range(len(dims))])
    return gain


def normal_values(stream_key, dims, scale, most, pieces=(), kind=jnp.bfloat16):
    array = scale * jax.random.normal(stream_key, dims, jnp.float32)
    if pieces:
        array = array * level_of(stream_key, dims, pieces, -0.22, 0.18)
    return jnp.clip(array, -most, most).astype(kind)


def setup_inputs(seed: int = 0, part: int = 0) -> dict:
    seeds = jax.random.split(jax.random.key(seed), 11)
    part_keys = jax.random.split(jax.random.fold_in(seeds[10], part), 11)
    fwd_prev = normal_values(part_keys[0], (SHOTS, NZ, NX, NY), 1.0, 6.0, ((0, 2), (1, 4), (2, 2)), jnp.float32)
    fwd_now = normal_values(part_keys[1], (SHOTS, NZ, NX, NY), 1.0, 6.0, ((0, 2), (1, 4), (2, 2)), jnp.float32)
    adj_late = normal_values(part_keys[2], (SHOTS, NZ, NX, NY), 1.0, 6.0, ((0, 2), (1, 4), (2, 2)), jnp.float32)
    adj_last = normal_values(part_keys[3], (SHOTS, NZ, NX, NY), 1.0, 6.0, ((0, 2), (1, 4), (2, 2)), jnp.float32)
    velocity = jnp.clip(1.5 + 3.0 * jax.random.uniform(part_keys[4], (NZ, NX, NY), jnp.float32) ** level_of(part_keys[4], (NZ, NX, NY), ((0, 4), (1, 2), (2, 2)), -0.2, 0.2), 1.5, 4.5)
    density = jnp.clip(1.5 + 1.0 * jax.random.uniform(part_keys[5], (NZ, NX, NY), jnp.float32) ** level_of(part_keys[5], (NZ, NX, NY), ((0, 4), (1, 2)), -0.2, 0.2), 1.5, 2.5)
    wavelet = normal_values(part_keys[6], (SHOTS, STEPS), 8.0, 48.0, ((0, 2),), jnp.float32)
    source_cell = place_ends(jax.random.randint(part_keys[7], (SHOTS,), 0, NZ * NX * NY), jax.random.fold_in(part_keys[7], 1), 0, (NZ * NX * NY) - 1).astype(jnp.int32)
    receiver_cell = place_ends(jax.random.randint(part_keys[8], (SHOTS, NREC), 0, NZ * NX * NY), jax.random.fold_in(part_keys[8], 1), 0, (NZ * NX * NY) - 1).astype(jnp.int32)
    observed = normal_values(part_keys[9], (SHOTS, STEPS, NREC), 3.0, 18.0, ((0, 2),), jnp.float32)
    return {"fwd_prev": fwd_prev, "fwd_now": fwd_now, "adj_late": adj_late, "adj_last": adj_last, "velocity": velocity, "density": density, "wavelet": wavelet, "source_cell": source_cell, "receiver_cell": receiver_cell, "observed": observed}


COURANT = 0.1
STEP_SIZE = 0.1
EPSILON = 1e-6
NEIGHBOURS = ((1, 0, 0), (-1, 0, 0), (0, 1, 0), (0, -1, 0), (0, 0, 1), (0, 0, -1))


def pad_cells(cells_array):
    widths = [(0, 0)] * (cells_array.ndim - 3) + [(1, 1)] * 3
    return jnp.pad(cells_array, widths)


def laplace(padded, buoy_pad):
    depth_cells = padded.shape[-3] - 2
    row_cells = padded.shape[-2] - 2
    col_cells = padded.shape[-1] - 2
    center_field = padded[..., 1:-1, 1:-1, 1:-1]
    center_buoy = buoy_pad[1:-1, 1:-1, 1:-1]
    summed = jnp.zeros(center_field.shape, jnp.float32)
    for shift_depth, shift_row, shift_col in NEIGHBOURS:
        near_buoy = buoy_pad[1 + shift_depth:1 + shift_depth + depth_cells, 1 + shift_row:1 + shift_row + row_cells, 1 + shift_col:1 + shift_col + col_cells]
        near_field = padded[..., 1 + shift_depth:1 + shift_depth + depth_cells, 1 + shift_row:1 + shift_row + row_cells, 1 + shift_col:1 + shift_col + col_cells]
        summed = summed + 0.5 * (center_buoy + near_buoy) * (near_field - center_field)
    return summed


def imaging(stiffness, buoy_pad, fwd_prev, fwd_now, adj_late, adj_last, wavelet, source_cell, receiver_cell, observed):
    def per_shot(gradient, shot_inputs):
        wave_prev, wave_now, late_adj, last_adj, amplitude, source_index, receiver_index, recorded = shot_inputs
        laplacians = []
        misfits = []
        for step_index in range(STEPS):
            laplacian = laplace(pad_cells(wave_now), buoy_pad)
            laplacians.append(laplacian)
            wave_next = 2.0 * wave_now - wave_prev + stiffness * laplacian
            flattened = wave_next.reshape(-1).at[source_index].add(amplitude[step_index])
            misfits.append(flattened[receiver_index] - recorded[step_index])
            wave_prev, wave_now = wave_now, flattened.reshape(wave_now.shape)
        for step_index in reversed(range(STEPS)):
            scaled = stiffness * last_adj
            adj_next = 2.0 * last_adj - late_adj + laplace(pad_cells(scaled), buoy_pad)
            adj_next = adj_next.reshape(-1).at[receiver_index].add(misfits[step_index]).reshape(last_adj.shape)
            gradient = gradient + adj_next * stiffness * laplacians[step_index]
            late_adj, last_adj = last_adj, adj_next
        return gradient, None

    start = jnp.zeros(stiffness.shape, jnp.float32)
    gradient, unused = lax.scan(per_shot, start, (fwd_prev, fwd_now, adj_late, adj_last, wavelet, source_cell, receiver_cell, observed))
    return gradient


def reference(fwd_prev, fwd_now, adj_late, adj_last, velocity, density, wavelet, source_cell, receiver_cell, observed):
    buoy_pad = pad_cells(1.0 / density)
    velocity_now = velocity
    direction = jnp.zeros(velocity.shape, jnp.float32)
    for update_index in range(ITERS):
        stiffness = (velocity_now * COURANT) ** 2 * density
        gradient = imaging(stiffness, buoy_pad, fwd_prev, fwd_now, adj_late, adj_last, wavelet, source_cell, receiver_cell, observed)
        largest = jnp.max(jnp.abs(gradient))
        direction = gradient / (largest + EPSILON)
        velocity_now = velocity_now * jnp.exp(-STEP_SIZE * direction)
    return velocity_now, direction
```

```python
import functools

import jax
import jax.numpy as jnp
from jax import lax
from jax.experimental import pallas as pl
from jax.experimental.pallas import tpu as pltpu
from jax.sharding import PartitionSpec as P

ITERS = 2
COURANT = 0.1
STEP_SIZE = 0.1
EPSILON = 1e-06
TILE = 8
MESH = pl.DeviceIdType.MESH


def split_index(value, size):
    if size & (size - 1) == 0:
        return lax.shift_right_logical(value, size.bit_length() - 1), value & (size - 1)
    return value // size, value % size


def roll_rows(block, edge, up):
    groups, depth, rows, cols = block.shape
    flat = pltpu.roll(block.reshape(groups * depth, rows, cols), rows - 1 if up else 1, 1)
    place = lax.broadcasted_iota(jnp.int32, flat.shape, 1)
    edge = jnp.broadcast_to(edge, (groups, depth, 1, cols)).reshape(groups * depth, 1, cols)
    return jnp.where(place == (rows - 1 if up else 0), edge, flat).reshape(block.shape)


def roll_cols(block, up):
    groups, depth, rows, cols = block.shape
    flat = pltpu.roll(block.reshape(groups * depth * rows, cols), cols - 1 if up else 1, 1)
    place = lax.broadcasted_iota(jnp.int32, flat.shape, 1)
    return jnp.where(place == (cols - 1 if up else 0), 0.0, flat).reshape(block.shape)


def neighbours(block, faces):
    zlo, zhi, rlo, rhi = faces
    return (
        jnp.concatenate([block[:, 1:], zhi], axis=1),
        jnp.concatenate([zlo, block[:, :-1]], axis=1),
        roll_rows(block, rhi, True),
        roll_rows(block, rlo, False),
        roll_cols(block, True),
        roll_cols(block, False),
    )


def laplace(block, faces, weights):
    total = None
    for near, weight in zip(neighbours(block, faces), weights):
        term = weight * (near - block)
        total = term if total is None else total + term
    return total


def kernel(
    sizes,
    fwd_prev,
    fwd_now,
    adj_late,
    adj_last,
    velocity,
    density,
    wavelet,
    source,
    receiver,
    observed,
    out_velocity,
    out_direction,
    wave_z,
    wave_r,
    model_z,
    model_r,
    wave_own,
    model_own,
    grad_own,
    grad_in,
    vel_in,
    vel_line,
    max_own,
    max_in,
    wave_send,
    wave_recv,
    model_send,
    model_recv,
    shot_send,
    shot_recv,
    max_send,
    max_recv,
):
    depth_n, shot_n, lat_n = sizes
    shots, depth, rows, cols = fwd_now.shape
    steps = observed.shape[1]
    count = receiver.shape[1]
    width = velocity.shape[2]
    me_z, me_s, me_l = lax.axis_index("depth"), lax.axis_index("shot"), lax.axis_index("lat")
    group = depth_n * lat_n
    me_g = me_z * lat_n + me_l

    def group_peer(offset):
        other = lax.rem(me_g + offset, group)
        return {"depth": other // lat_n, "lat": lax.rem(other, lat_n)}

    def shot_peer(offset):
        return {"shot": lax.rem(me_s + offset, shot_n)}

    barrier = pltpu.get_barrier_semaphore()
    for offset in range(1, group):
        pl.semaphore_signal(barrier, inc=1, device_id=group_peer(offset), device_id_type=MESH)
    for offset in range(1, shot_n):
        pl.semaphore_signal(barrier, inc=1, device_id=shot_peer(offset), device_id_type=MESH)
    pl.semaphore_wait(barrier, group - 1 + shot_n - 1)

    sides = (
        (me_z > 0, {"depth": me_z - 1}, me_z < depth_n - 1),
        (me_z < depth_n - 1, {"depth": me_z + 1}, me_z > 0),
        (me_l > 0, {"lat": me_l - 1}, me_l < lat_n - 1),
        (me_l < lat_n - 1, {"lat": me_l + 1}, me_l > 0),
    )

    def face_copies(src, zbuf, rbuf, send, recv, slot):
        refs = (
            (src.at[:, 0:1], zbuf.at[slot, 1]),
            (src.at[:, depth - 1 : depth], zbuf.at[slot, 0]),
            (src.at[:, :, 0:TILE], rbuf.at[slot, 1]),
            (src.at[:, :, rows - TILE : rows], rbuf.at[slot, 0]),
        )
        return [
            pltpu.make_async_remote_copy(
                src_ref=here,
                dst_ref=there,
                send_sem=send.at[slot, way],
                recv_sem=recv.at[slot, way],
                device_id=sides[way][1],
                device_id_type=MESH,
            )
            for way, (here, there) in enumerate(refs)
        ]

    pending = []

    def start_faces(src, is_wave, slot):
        if is_wave:
            copies = face_copies(src, wave_z, wave_r, wave_send, wave_recv, slot)
        else:
            copies = face_copies(src, model_z, model_r, model_send, model_recv, slot)
        for way, copy in enumerate(copies):
            pl.when(sides[way][0])(copy.start)
            pending.append((sides[way][0], copy))
        return copies

    def wait_faces(copies):
        for way, copy in enumerate(copies):
            pl.when(sides[way][2])(copy.wait_recv)

    def read_faces(is_wave, slot):
        zbuf, rbuf = (wave_z, wave_r) if is_wave else (model_z, model_r)
        return (
            jnp.where(me_z > 0, zbuf[slot, 0], 0.0),
            jnp.where(me_z < depth_n - 1, zbuf[slot, 1], 0.0),
            jnp.where(me_l > 0, rbuf[slot, 0][:, :, TILE - 1 : TILE], 0.0),
            jnp.where(me_l < lat_n - 1, rbuf[slot, 1][:, :, 0:1], 0.0),
        )

    def shot_copies(src, buffer, slot):
        return [
            pltpu.make_async_remote_copy(
                src_ref=src,
                dst_ref=buffer.at[offset - 1],
                send_sem=shot_send.at[slot, offset - 1],
                recv_sem=shot_recv.at[slot, offset - 1],
                device_id=shot_peer(offset),
                device_id_type=MESH,
            )
            for offset in range(1, shot_n)
        ]

    vel_copies = shot_copies(velocity, vel_in, 0)
    for copy in vel_copies:
        copy.start()
    density_copies = start_faces(density, False, 0)
    now_copies = start_faces(fwd_now, True, 0)
    last_copies = start_faces(adj_last, True, 1)

    plane_start = me_z * depth
    row_start = me_l * rows
    full_rows = rows * lat_n
    counts = []
    records = [[] for unused in range(steps)]
    row_place = lax.broadcasted_iota(jnp.int32, (depth * rows, count), 0)
    col_place = lax.broadcasted_iota(jnp.int32, (cols, count), 0)
    for shot in range(shots):
        line, col = split_index(receiver[shot : shot + 1, :], cols)
        plane, row = split_index(line, full_rows)
        plane = plane - plane_start
        row = row - row_start
        inside = (plane >= 0) & (plane < depth) & (row >= 0) & (row < rows)
        place = jnp.where(inside, plane * rows + row, -1)
        picks = jnp.where(row_place == place, 1.0, 0.0)
        col_picks = jnp.where(col_place == col, 1.0, 0.0).astype(jnp.bfloat16)

        def spread(values, picks=picks, col_picks=col_picks):
            left = picks if values is None else picks * values
            return lax.dot_general(
                left.astype(jnp.bfloat16),
                col_picks,
                (((1,), (1,)), ((), ())),
                preferred_element_type=jnp.float32,
            )

        counts.append(spread(None).reshape(1, depth, rows, cols))
        for step in range(steps):
            value = observed[shot, step : step + 1, :]
            high = value.astype(jnp.bfloat16).astype(jnp.float32)
            middle = (value - high).astype(jnp.bfloat16).astype(jnp.float32)
            low = value - high - middle
            total = spread(high) + (spread(middle) + spread(low))
            records[step].append(total.reshape(1, depth, rows, cols))
    counts = jnp.concatenate(counts, axis=0)
    records = [jnp.concatenate(record, axis=0) for record in records]

    spot = (1, depth, rows, cols)
    cell_index = (
        (lax.broadcasted_iota(jnp.int32, spot, 1) + plane_start) * full_rows
        + lax.broadcasted_iota(jnp.int32, spot, 2)
        + row_start
    ) * cols + lax.broadcasted_iota(jnp.int32, spot, 3)
    hits = [cell_index == source[shot] for shot in range(shots)]

    def sources(step):
        return jnp.concatenate(
            [jnp.where(hits[shot], wavelet[shot, step], 0.0) for shot in range(shots)], axis=0
        )

    def placed(piece, owner):
        vel_line[:, :, 0:width] = piece
        line = vel_line[...].reshape(depth * rows, cols)
        return pltpu.roll(line, owner * width, 1).reshape(depth, rows, cols)

    vel_line[...] = jnp.zeros_like(vel_line)
    speed = placed(velocity[...], me_s)
    for offset in range(1, shot_n):
        vel_copies[offset - 1].wait_recv()
        speed = speed + placed(vel_in[offset - 1], lax.rem(me_s + shot_n - offset, shot_n))

    wait_faces(density_copies)
    own_density = density[...]
    dens_faces = read_faces(False, 0)
    valid = (me_z > 0, me_z < depth_n - 1, me_l > 0, me_l < lat_n - 1)
    buoy = 1.0 / own_density
    buoy_faces = tuple(
        jnp.where(ok, 1.0 / jnp.where(ok, face, 1.0), 0.0) for ok, face in zip(valid, dens_faces)
    )
    weights = [0.5 * (buoy + near) for near in neighbours(buoy, buoy_faces)]

    wait_faces(now_copies)
    first = fwd_now[...]
    before = fwd_prev[...]
    first_lap = laplace(first, read_faces(True, 0), weights)
    wait_faces(last_copies)
    last = adj_last[...]
    late = adj_late[...]
    last_faces = read_faces(True, 1)

    direction = None
    wave_slot = 2
    for update in range(ITERS):
        stiff = (speed[None] * COURANT) ** 2 * own_density
        model_own[update] = stiff
        stiff_copies = start_faces(model_own.at[update], False, 1 + update)
        laps = []
        misfits = []
        wave_prev, wave_now = before, first
        for step in range(steps):
            if step == 0:
                lap = first_lap
            else:
                wait_faces(wave_copies)
                lap = laplace(wave_now, read_faces(True, wave_slot - 1), weights)
            wave_next = 2.0 * wave_now - wave_prev + stiff * lap + sources(step)
            if step < steps - 1:
                wave_own[wave_slot - 2] = wave_next
                wave_copies = start_faces(wave_own.at[wave_slot - 2], True, wave_slot)
                wave_slot += 1
            laps.append(lap)
            misfits.append(counts * wave_next - records[step])
            wave_prev, wave_now = wave_now, wave_next
            if step == 0:
                wait_faces(stiff_copies)
                stiff_faces = read_faces(False, 1 + update)
                scaled = stiff * last
                scaled_faces = tuple(a * b for a, b in zip(stiff_faces, last_faces))
                scaled_lap = laplace(scaled, scaled_faces, weights)
        gradient = None
        adj_late_now, adj_now = late, last
        for step in reversed(range(steps)):
            if step < steps - 1:
                wait_faces(wave_copies)
                scaled_lap = laplace(scaled, read_faces(True, wave_slot - 1), weights)
            adj_next = 2.0 * adj_now - adj_late_now + scaled_lap + misfits[step]
            scaled = stiff * adj_next
            if step > 0:
                wave_own[wave_slot - 2] = scaled
                wave_copies = start_faces(wave_own.at[wave_slot - 2], True, wave_slot)
                wave_slot += 1
            term = jnp.sum(scaled * laps[step], axis=0)
            gradient = term if gradient is None else gradient + term
            adj_late_now, adj_now = adj_now, adj_next
        grad_own[update] = gradient
        grad_copies = shot_copies(grad_own.at[update], grad_in.at[update], 1 + update)
        for copy in grad_copies:
            copy.start()
        for offset, copy in enumerate(grad_copies):
            copy.wait_recv()
            gradient = gradient + grad_in[update, offset]
        top = jnp.max(jnp.abs(gradient).reshape(-1, TILE, cols), axis=0)
        max_own[update] = top
        max_copies = [
            pltpu.make_async_remote_copy(
                src_ref=max_own.at[update],
                dst_ref=max_in.at[update, offset - 1],
                send_sem=max_send.at[update, offset - 1],
                recv_sem=max_recv.at[update, offset - 1],
                device_id=group_peer(offset),
                device_id_type=MESH,
            )
            for offset in range(1, group)
        ]
        for copy in max_copies:
            copy.start()
        for offset, copy in enumerate(max_copies):
            copy.wait_recv()
            top = jnp.maximum(top, max_in[update, offset])
        largest = jnp.max(top)
        direction = gradient / (largest + EPSILON)
        speed = speed * jnp.exp(-STEP_SIZE * direction)
        for copy in grad_copies + max_copies:
            copy.wait_send()

    def own_lines(block):
        flat = block.reshape(depth * rows, cols)
        turned = pltpu.roll(flat, lax.rem(cols - me_s * width, cols), 1)
        return turned[:, 0:width].reshape(depth, rows, width)

    out_velocity[...] = own_lines(speed)
    out_direction[...] = own_lines(direction)
    for copy in vel_copies:
        copy.wait_send()
    for going, copy in pending:
        pl.when(going)(copy.wait_send)


def shards(sizes, *arrays):
    velocity = arrays[4]
    shots, depth, rows, cols = arrays[1].shape
    steps = arrays[6].shape[1]
    depth_n, shot_n, lat_n = sizes
    arrays = list(arrays)
    arrays[5] = arrays[5][None]
    waves = 2 + ITERS * 2 * (steps - 1)
    models = 1 + ITERS
    group = depth_n * lat_n
    f32 = jnp.float32
    dma = pltpu.SemaphoreType.DMA
    vmem = pl.BlockSpec(memory_space=pltpu.VMEM)
    smem = pl.BlockSpec(memory_space=pltpu.SMEM)
    peers = max(shot_n - 1, 1)
    others = max(group - 1, 1)
    out = jax.ShapeDtypeStruct(velocity.shape, f32)
    return pl.pallas_call(
        functools.partial(kernel, sizes),
        out_shape=(out, out),
        in_specs=[vmem] * 6 + [smem] * 2 + [vmem] * 2,
        out_specs=(vmem, vmem),
        scratch_shapes=[
            pltpu.VMEM((waves, 2, shots, 1, rows, cols), f32),
            pltpu.VMEM((waves, 2, shots, depth, TILE, cols), f32),
            pltpu.VMEM((models, 2, 1, 1, rows, cols), f32),
            pltpu.VMEM((models, 2, 1, depth, TILE, cols), f32),
            pltpu.VMEM((max(waves - 2, 1), shots, depth, rows, cols), f32),
            pltpu.VMEM((ITERS, 1, depth, rows, cols), f32),
            pltpu.VMEM((ITERS, depth, rows, cols), f32),
            pltpu.VMEM((ITERS, peers, depth, rows, cols), f32),
            pltpu.VMEM((peers,) + velocity.shape, f32),
            pltpu.VMEM((depth, rows, cols), f32),
            pltpu.VMEM((ITERS, TILE, cols), f32),
            pltpu.VMEM((ITERS, others, TILE, cols), f32),
            dma((waves, 4)),
            dma((waves, 4)),
            dma((models, 4)),
            dma((models, 4)),
            dma((1 + ITERS, peers)),
            dma((1 + ITERS, peers)),
            dma((ITERS, others)),
            dma((ITERS, others)),
        ],
        compiler_params=pltpu.CompilerParams(
            collective_id=0, has_side_effects=True, vmem_limit_bytes=32 * 1024 * 1024
        ),
    )(*arrays)


def solution(mesh):
    sizes = (mesh.shape["depth"], mesh.shape["shot"], mesh.shape["lat"])
    placed = (
        P(("grp", "shot"), "depth", "lat", None),
        P(("grp", "shot"), "depth", "lat", None),
        P(("grp", "shot"), "depth", "lat", None),
        P(("grp", "shot"), "depth", "lat", None),
        P(("grp", "depth"), "lat", "shot"),
        P(("grp", "depth"), "lat", None),
        P(("grp", "shot"), None),
        P(("grp", "shot")),
        P(("grp", "shot"), None),
        P(("grp", "shot"), None, None),
    )
    return jax.shard_map(
        functools.partial(shards, sizes),
        mesh=mesh,
        in_specs=placed,
        out_specs=(P(("grp", "depth"), "lat", "shot"), P(("grp", "depth"), "lat", "shot")),
        check_vma=False,
    )
```

```python
import functools

import jax
import jax.numpy as jnp
from jax import lax
from jax.experimental import pallas as pl
from jax.experimental.pallas import tpu as pltpu
from jax.sharding import PartitionSpec as P

ITERS = 2
COURANT = 0.1
STEP_SIZE = 0.1
EPSILON = 1e-06
TILE = 8
MESH = pl.DeviceIdType.MESH


def split_index(value, size):
    if size & (size - 1) == 0:
        return lax.shift_right_logical(value, size.bit_length() - 1), value & (size - 1)
    return value // size, value % size


def roll_rows(block, edge, up):
    groups, depth, rows, cols = block.shape
    flat = pltpu.roll(block.reshape(groups * depth, rows, cols), rows - 1 if up else 1, 1)
    place = lax.broadcasted_iota(jnp.int32, flat.shape, 1)
    edge = jnp.broadcast_to(edge, (groups, depth, 1, cols)).reshape(groups * depth, 1, cols)
    return jnp.where(place == (rows - 1 if up else 0), edge, flat).reshape(block.shape)


def roll_cols(block, up):
    groups, depth, rows, cols = block.shape
    flat = pltpu.roll(block.reshape(groups * depth * rows, cols), cols - 1 if up else 1, 1)
    place = lax.broadcasted_iota(jnp.int32, flat.shape, 1)
    return jnp.where(place == (cols - 1 if up else 0), 0.0, flat).reshape(block.shape)


def neighbours(block, faces):
    zlo, zhi, rlo, rhi = faces
    return (
        jnp.concatenate([block[:, 1:], zhi], axis=1),
        jnp.concatenate([zlo, block[:, :-1]], axis=1),
        roll_rows(block, rhi, True),
        roll_rows(block, rlo, False),
        roll_cols(block, True),
        roll_cols(block, False),
    )


def inner_laplace(block, weights):
    depth_zero = jnp.zeros_like(block[:, 0:1])
    row_zero = jnp.zeros_like(block[:, :, 0:1])
    return laplace(block, (depth_zero, depth_zero, row_zero, row_zero), weights)


def add_faces(inner, faces, weights):
    zlo, zhi, rlo, rhi = faces
    high, low, up, down = weights[:4]
    depth, rows = inner.shape[1:3]
    place = lax.broadcasted_iota(jnp.int32, (1, 1, TILE, inner.shape[3]), 2)
    first = inner[:, :, :TILE] + jnp.where(place == 0, down[:, :, :TILE] * rlo, 0.0)
    inner = jnp.concatenate([first, inner[:, :, TILE:]], axis=2)
    last = inner[:, :, rows - TILE :]
    last = last + jnp.where(place == TILE - 1, up[:, :, rows - TILE :] * rhi, 0.0)
    inner = jnp.concatenate([inner[:, :, : rows - TILE], last], axis=2)
    inner = jnp.concatenate([inner[:, :1] + low[:, :1] * zlo, inner[:, 1:]], axis=1)
    last = inner[:, depth - 1 :] + high[:, depth - 1 :] * zhi
    return jnp.concatenate([inner[:, : depth - 1], last], axis=1) if depth > 1 else last


def laplace(block, faces, weights):
    total = None
    for near, weight in zip(neighbours(block, faces), weights):
        term = weight * (near - block)
        total = term if total is None else total + term
    return total


def kernel(
    sizes,
    fwd_prev_hbm,
    fwd_now_hbm,
    adj_late_hbm,
    adj_last_hbm,
    velocity_hbm,
    density_hbm,
    wavelet_hbm,
    source_hbm,
    receiver_hbm,
    observed_hbm,
    out_pair,
    fwd_prev,
    fwd_now,
    adj_late,
    adj_last,
    velocity,
    density,
    wavelet,
    source,
    receiver,
    observed,
    load_sem,
    wave_z,
    wave_r,
    model_z,
    model_r,
    wave_own,
    model_own,
    grad_own,
    grad_in,
    vel_in,
    vel_line,
    max_own,
    max_in,
    wave_send,
    wave_recv,
    model_send,
    model_recv,
    shot_send,
    shot_recv,
    max_send,
    max_recv,
):
    depth_n, shot_n, lat_n = sizes
    shots, depth, rows, cols = fwd_now.shape
    steps = observed.shape[1]
    count = receiver.shape[1]
    width = velocity.shape[2]
    me_z, me_s, me_l = lax.axis_index("depth"), lax.axis_index("shot"), lax.axis_index("lat")
    group = depth_n * lat_n
    me_g = me_z * lat_n + me_l

    def group_peer(offset):
        other = lax.rem(me_g + offset, group)
        return {"depth": other // lat_n, "lat": lax.rem(other, lat_n)}

    def shot_peer(offset):
        return {"shot": lax.rem(me_s + offset, shot_n)}

    loads = {}
    for place, (name, there, here) in enumerate(
        (
            ("receiver", receiver_hbm, receiver),
            ("observed", observed_hbm, observed),
            ("velocity", velocity_hbm, velocity),
            ("density", density_hbm, density),
            ("fwd_now", fwd_now_hbm, fwd_now),
            ("fwd_prev", fwd_prev_hbm, fwd_prev),
            ("adj_last", adj_last_hbm, adj_last),
            ("adj_late", adj_late_hbm, adj_late),
            ("wavelet", wavelet_hbm, wavelet),
            ("source", source_hbm, source),
        )
    ):
        loads[name] = pltpu.make_async_copy(there, here, load_sem.at[place])
        loads[name].start()

    barrier = pltpu.get_barrier_semaphore()
    for offset in range(1, group):
        pl.semaphore_signal(barrier, inc=1, device_id=group_peer(offset), device_id_type=MESH)
    for offset in range(1, shot_n):
        pl.semaphore_signal(barrier, inc=1, device_id=shot_peer(offset), device_id_type=MESH)
    pl.semaphore_wait(barrier, group - 1 + shot_n - 1)

    sides = (
        (me_z > 0, {"depth": me_z - 1}, me_z < depth_n - 1),
        (me_z < depth_n - 1, {"depth": me_z + 1}, me_z > 0),
        (me_l > 0, {"lat": me_l - 1}, me_l < lat_n - 1),
        (me_l < lat_n - 1, {"lat": me_l + 1}, me_l > 0),
    )

    def face_copies(src, zbuf, rbuf, send, recv, slot):
        refs = (
            (src.at[:, 0:1], zbuf.at[slot, 1]),
            (src.at[:, depth - 1 : depth], zbuf.at[slot, 0]),
            (src.at[:, :, 0:TILE], rbuf.at[slot, 1]),
            (src.at[:, :, rows - TILE : rows], rbuf.at[slot, 0]),
        )
        return [
            pltpu.make_async_remote_copy(
                src_ref=here,
                dst_ref=there,
                send_sem=send.at[slot, way],
                recv_sem=recv.at[slot, way],
                device_id=sides[way][1],
                device_id_type=MESH,
            )
            for way, (here, there) in enumerate(refs)
        ]

    pending = []

    def start_faces(src, is_wave, slot):
        if is_wave:
            copies = face_copies(src, wave_z, wave_r, wave_send, wave_recv, slot)
        else:
            copies = face_copies(src, model_z, model_r, model_send, model_recv, slot)
        for way, copy in enumerate(copies):
            pl.when(sides[way][0])(copy.start)
            pending.append((sides[way][0], copy))
        return copies

    def wait_faces(copies):
        for way, copy in enumerate(copies):
            pl.when(sides[way][2])(copy.wait_recv)

    def read_faces(is_wave, slot):
        zbuf, rbuf = (wave_z, wave_r) if is_wave else (model_z, model_r)
        return (
            jnp.where(me_z > 0, zbuf[slot, 0], 0.0),
            jnp.where(me_z < depth_n - 1, zbuf[slot, 1], 0.0),
            jnp.where(me_l > 0, rbuf[slot, 0][:, :, TILE - 1 : TILE], 0.0),
            jnp.where(me_l < lat_n - 1, rbuf[slot, 1][:, :, 0:1], 0.0),
        )

    def shot_copies(src, buffer, slot):
        return [
            pltpu.make_async_remote_copy(
                src_ref=src,
                dst_ref=buffer.at[offset - 1],
                send_sem=shot_send.at[slot, offset - 1],
                recv_sem=shot_recv.at[slot, offset - 1],
                device_id=shot_peer(offset),
                device_id_type=MESH,
            )
            for offset in range(1, shot_n)
        ]

    vel_copies = shot_copies(velocity_hbm, vel_in, 0)
    for copy in vel_copies:
        copy.start()
    density_copies = start_faces(density_hbm, False, 0)
    now_copies = start_faces(fwd_now_hbm, True, 0)
    last_copies = start_faces(adj_last_hbm, True, 1)
    loads["receiver"].wait()
    loads["observed"].wait()

    plane_start = me_z * depth
    row_start = me_l * rows
    full_rows = rows * lat_n
    counts = []
    records = [[] for unused in range(steps)]
    row_place = lax.broadcasted_iota(jnp.int32, (depth * rows, count), 0)
    col_place = lax.broadcasted_iota(jnp.int32, (cols, count), 0)
    for shot in range(shots):
        line, col = split_index(receiver[shot : shot + 1, :], cols)
        plane, row = split_index(line, full_rows)
        plane = plane - plane_start
        row = row - row_start
        inside = (plane >= 0) & (plane < depth) & (row >= 0) & (row < rows)
        place = jnp.where(inside, plane * rows + row, -1)
        picks = jnp.where(row_place == place, 1.0, 0.0)
        col_picks = jnp.where(col_place == col, 1.0, 0.0).astype(jnp.bfloat16)

        def spread(values, picks=picks, col_picks=col_picks):
            left = picks if values is None else picks * values
            return lax.dot_general(
                left.astype(jnp.bfloat16),
                col_picks,
                (((1,), (1,)), ((), ())),
                preferred_element_type=jnp.float32,
            )

        counts.append(spread(None).reshape(1, depth, rows, cols))
        for step in range(steps):
            value = observed[shot, step : step + 1, :]
            high = value.astype(jnp.bfloat16).astype(jnp.float32)
            middle = (value - high).astype(jnp.bfloat16).astype(jnp.float32)
            low = value - high - middle
            total = spread(high) + (spread(middle) + spread(low))
            records[step].append(total.reshape(1, depth, rows, cols))
    counts = jnp.concatenate(counts, axis=0)
    records = [jnp.concatenate(record, axis=0) for record in records]

    spot = (1, depth, rows, cols)
    cell_index = (
        (lax.broadcasted_iota(jnp.int32, spot, 1) + plane_start) * full_rows
        + lax.broadcasted_iota(jnp.int32, spot, 2)
        + row_start
    ) * cols + lax.broadcasted_iota(jnp.int32, spot, 3)
    loads["source"].wait()
    loads["wavelet"].wait()
    hits = [cell_index == source[shot] for shot in range(shots)]

    def sources(step):
        return jnp.concatenate(
            [jnp.where(hits[shot], wavelet[shot, step], 0.0) for shot in range(shots)], axis=0
        )

    def placed(piece, owner):
        vel_line[:, :, 0:width] = piece
        line = vel_line[...].reshape(depth * rows, cols)
        return pltpu.roll(line, owner * width, 1).reshape(depth, rows, cols)

    vel_line[...] = jnp.zeros_like(vel_line)
    loads["velocity"].wait()
    speed = placed(velocity[...], me_s)
    for offset in range(1, shot_n):
        vel_copies[offset - 1].wait_recv()
        speed = speed + placed(vel_in[offset - 1], lax.rem(me_s + shot_n - offset, shot_n))

    model_own[0] = speed[None]
    speed_copies = start_faces(model_own.at[0], False, 1)
    wait_faces(density_copies)
    loads["density"].wait()
    own_density = density[...]
    dens_faces = read_faces(False, 0)
    valid = (me_z > 0, me_z < depth_n - 1, me_l > 0, me_l < lat_n - 1)
    buoy = 1.0 / own_density
    buoy_faces = tuple(
        jnp.where(ok, 1.0 / jnp.where(ok, face, 1.0), 0.0) for ok, face in zip(valid, dens_faces)
    )
    weights = [0.5 * (buoy + near) for near in neighbours(buoy, buoy_faces)]

    loads["fwd_now"].wait()
    loads["fwd_prev"].wait()
    first = fwd_now[...]
    before = fwd_prev[...]
    inner = inner_laplace(first, weights)
    wait_faces(now_copies)
    first_lap = add_faces(inner, read_faces(True, 0), weights)
    loads["adj_last"].wait()
    loads["adj_late"].wait()
    last = adj_last[...]
    late = adj_late[...]

    direction = None
    wave_slot = 2
    for update in range(ITERS):
        stiff = (speed[None] * COURANT) ** 2 * own_density
        if update > 0:
            stiff_faces = tuple(
                (face * COURANT) ** 2 * near for face, near in zip(speed_faces, dens_faces)
            )
        laps = []
        misfits = []
        wave_prev, wave_now = before, first
        for step in range(steps):
            if step == 0:
                lap = first_lap
            elif step == 1 and update == 0:
                wait_faces(wave_copies)
                second_faces = read_faces(True, second_slot)
                lap = add_faces(inner, second_faces, weights)
            elif step == 1:
                if update == 1:
                    wait_faces(lap_copies)
                    lap_faces = read_faces(True, second_slot + 1)
                near = tuple(
                    old + (stiff_face - stiff_old) * lap_face
                    for old, stiff_face, stiff_old, lap_face in zip(
                        second_faces, stiff_faces, first_stiff_faces, lap_faces
                    )
                )
                lap = add_faces(inner, near, weights)
            else:
                wait_faces(wave_copies)
                lap = add_faces(inner, read_faces(True, wave_slot - 1), weights)
            wave_next = 2.0 * wave_now - wave_prev + stiff * lap + sources(step)
            if step < steps - 1 and (step > 0 or update == 0):
                wave_own[wave_slot - 2] = wave_next
                wave_copies = start_faces(wave_own.at[wave_slot - 2], True, wave_slot)
                wave_slot += 1
                if step == 0:
                    second_slot = wave_slot - 1
                    wave_own[wave_slot - 2] = first_lap
                    lap_copies = start_faces(wave_own.at[wave_slot - 2], True, wave_slot)
                    wave_slot += 1
            if step < steps - 1:
                inner = inner_laplace(wave_next, weights)
            laps.append(lap)
            misfits.append(counts * wave_next - records[step])
            wave_prev, wave_now = wave_now, wave_next
            if step == 0:
                scaled = stiff * last
                scaled_lap = inner_laplace(scaled, weights)
                if update == 0:
                    wait_faces(speed_copies)
                    speed_faces = read_faces(False, 1)
                    stiff_faces = tuple(
                        (face * COURANT) ** 2 * near for face, near in zip(speed_faces, dens_faces)
                    )
                    first_stiff_faces = stiff_faces
                    wait_faces(last_copies)
                    last_faces = read_faces(True, 1)
                scaled_faces = tuple(a * b for a, b in zip(stiff_faces, last_faces))
                scaled_lap = add_faces(scaled_lap, scaled_faces, weights)
        gradient = None
        adj_late_now, adj_now = late, last
        for step in reversed(range(steps)):
            adj_next = 2.0 * adj_now - adj_late_now + scaled_lap + misfits[step]
            if step < steps - 1:
                wait_faces(wave_copies)
                adj_next = add_faces(adj_next, read_faces(True, wave_slot - 1), weights)
            scaled = stiff * adj_next
            if step > 0:
                wave_own[wave_slot - 2] = scaled
                wave_copies = start_faces(wave_own.at[wave_slot - 2], True, wave_slot)
                wave_slot += 1
            if step > 0:
                scaled_lap = inner_laplace(scaled, weights)
            term = jnp.sum(scaled * laps[step], axis=0)
            gradient = term if gradient is None else gradient + term
            adj_late_now, adj_now = adj_now, adj_next
        grad_own[update] = gradient
        grad_copies = shot_copies(grad_own.at[update], grad_in.at[update], 1 + update)
        for copy in grad_copies:
            copy.start()
        for offset, copy in enumerate(grad_copies):
            copy.wait_recv()
            gradient = gradient + grad_in[update, offset]
        top = jnp.max(jnp.abs(gradient).reshape(-1, TILE, cols), axis=0)
        max_own[update] = top
        max_copies = [
            pltpu.make_async_remote_copy(
                src_ref=max_own.at[update],
                dst_ref=max_in.at[update, offset - 1],
                send_sem=max_send.at[update, offset - 1],
                recv_sem=max_recv.at[update, offset - 1],
                device_id=group_peer(offset),
                device_id_type=MESH,
            )
            for offset in range(1, group)
        ]
        for copy in max_copies:
            copy.start()
        if update < ITERS - 1:
            model_own[1 + update] = gradient[None]
            side_copies = start_faces(model_own.at[1 + update], False, 2 + update)
        for offset, copy in enumerate(max_copies):
            copy.wait_recv()
            top = jnp.maximum(top, max_in[update, offset])
        largest = jnp.max(top)
        direction = gradient / (largest + EPSILON)
        speed = speed * jnp.exp(-STEP_SIZE * direction)
        if update < ITERS - 1:
            wait_faces(side_copies)
            speed_faces = tuple(
                face * jnp.exp(-STEP_SIZE * (side / (largest + EPSILON)))
                for face, side in zip(speed_faces, read_faces(False, 2 + update))
            )
        for copy in grad_copies + max_copies:
            copy.wait_send()

    def own_lines(block):
        flat = block.reshape(depth * rows, cols)
        turned = pltpu.roll(flat, lax.rem(cols - me_s * width, cols), 1)
        return turned[:, 0:width].reshape(depth, rows, width)

    out_pair[0] = own_lines(speed)
    out_pair[1] = own_lines(direction)
    for copy in vel_copies:
        copy.wait_send()
    for going, copy in pending:
        pl.when(going)(copy.wait_send)


def finish(pair, out_velocity, out_direction, sems):
    copies = [
        pltpu.make_async_copy(pair.at[0], out_velocity, sems.at[0]),
        pltpu.make_async_copy(pair.at[1], out_direction, sems.at[1]),
    ]
    for copy in copies:
        copy.start()
    for copy in copies:
        copy.wait()


def shards(sizes, *arrays):
    velocity = arrays[4]
    shots, depth, rows, cols = arrays[1].shape
    steps = arrays[6].shape[1]
    depth_n, shot_n, lat_n = sizes
    arrays = list(arrays)
    arrays[5] = arrays[5][None]
    waves = 4 + ITERS * 2 * (steps - 1) - ITERS
    models = 1 + ITERS
    group = depth_n * lat_n
    f32 = jnp.float32
    dma = pltpu.SemaphoreType.DMA
    vmem = pl.BlockSpec(memory_space=pltpu.VMEM)
    hbm = pl.BlockSpec(memory_space=pltpu.HBM)
    held = [
        (pltpu.SMEM if place in (6, 7) else pltpu.VMEM)(array.shape, array.dtype)
        for place, array in enumerate(arrays)
    ]
    peers = max(shot_n - 1, 1)
    others = max(group - 1, 1)
    out = jax.ShapeDtypeStruct(velocity.shape, f32)
    pair = pl.pallas_call(
        functools.partial(kernel, sizes),
        out_shape=jax.ShapeDtypeStruct((2,) + velocity.shape, f32),
        in_specs=[hbm] * len(arrays),
        out_specs=vmem,
        scratch_shapes=held
        + [
            dma((len(arrays),)),
            pltpu.VMEM((waves, 2, shots, 1, rows, cols), f32),
            pltpu.VMEM((waves, 2, shots, depth, TILE, cols), f32),
            pltpu.VMEM((models, 2, 1, 1, rows, cols), f32),
            pltpu.VMEM((models, 2, 1, depth, TILE, cols), f32),
            pltpu.VMEM((max(waves - 2, 1), shots, depth, rows, cols), f32),
            pltpu.VMEM((ITERS, 1, depth, rows, cols), f32),
            pltpu.VMEM((ITERS, depth, rows, cols), f32),
            pltpu.VMEM((ITERS, peers, depth, rows, cols), f32),
            pltpu.VMEM((peers,) + velocity.shape, f32),
            pltpu.VMEM((depth, rows, cols), f32),
            pltpu.VMEM((ITERS, TILE, cols), f32),
            pltpu.VMEM((ITERS, others, TILE, cols), f32),
            dma((waves, 4)),
            dma((waves, 4)),
            dma((models, 4)),
            dma((models, 4)),
            dma((1 + ITERS, peers)),
            dma((1 + ITERS, peers)),
            dma((ITERS, others)),
            dma((ITERS, others)),
        ],
        compiler_params=pltpu.CompilerParams(
            collective_id=0, has_side_effects=True, vmem_limit_bytes=60 * 1024 * 1024
        ),
    )(*arrays)
    return pl.pallas_call(
        finish,
        out_shape=(out, out),
        in_specs=[vmem],
        out_specs=(hbm, hbm),
        scratch_shapes=[dma((2,))],
        compiler_params=pltpu.CompilerParams(has_side_effects=True),
    )(pair)


def solution(mesh):
    sizes = (mesh.shape["depth"], mesh.shape["shot"], mesh.shape["lat"])
    placed = (
        P(("grp", "shot"), "depth", "lat", None),
        P(("grp", "shot"), "depth", "lat", None),
        P(("grp", "shot"), "depth", "lat", None),
        P(("grp", "shot"), "depth", "lat", None),
        P(("grp", "depth"), "lat", "shot"),
        P(("grp", "depth"), "lat", None),
        P(("grp", "shot"), None),
        P(("grp", "shot")),
        P(("grp", "shot"), None),
        P(("grp", "shot"), None, None),
    )
    return jax.shard_map(
        functools.partial(shards, sizes),
        mesh=mesh,
        in_specs=placed,
        out_specs=(P(("grp", "depth"), "lat", "shot"), P(("grp", "depth"), "lat", "shot")),
        check_vma=False,
    )
```
